32 devices in a mesh: seq: 32 (over z, y, x, core), dp: 1.
Axes of the slice: x: 2, y: 2, z: 4, core: 2. Of those that a mesh axis runs over, the one named last changes fastest.
Arguments:
- tokens: bfloat16 [1, 16384, 1536], P('dp', 'seq'), may hold values from -6 to 6
- cotangent: bfloat16 [1, 16384, 1536], P('dp', 'seq'), may hold values from -6 to 6
- conv_weight: float32 [3, 1536], replicated, may hold values from -3.5 to 3.5
- gate_weight: bfloat16 [1536, 1536], P('seq'), may hold values from -0.15625 to 0.15625
- leading_block_factor: bfloat16 [128, 128, 128], P('seq'), may hold values from -0.5 to 0.5
- trailing_block_factor: bfloat16 [128, 128, 128], P('seq'), may hold values from -0.5 to 0.5
Outputs:
- mixed: bfloat16 [1, 16384, 1536], P('dp', 'seq')
- grad_tokens: bfloat16 [1, 16384, 1536], P('dp', 'seq')
- grad_conv: float32 [3, 1536], replicated
- grad_gate: float32 [1536, 1536], P('seq')
- grad_first: float32 [128, 128, 128], P('seq')
- trailing_factor_gradient: float32 [128, 128, 128], P('seq')
The draws below stay inside these ranges and needn't reach their ends.
All inputs are finite; a program needn't handle non-finite values.
Results may differ from the reference program's by a relative error of at most 0.0067.
Values may be sent and summed in bfloat16 or wider, within the bound.
A program may use at most 128 MiB of HBM per device.

```python
import jax
import jax.numpy as jnp
from jax import lax

D = 1536
BS = 128
L = 16384
NB = 128
DOCS = 1


def with_spikes(entries, rng, source, target, shards_of, factor):
    def block_of(axis_at):
        return (jnp.arange(entries.shape[axis_at]) // (entries.shape[axis_at] // shards_of)).reshape((-1,) + (1,) * (entries.ndim - 1 - axis_at))

    near = jax.random.permutation(rng, shards_of)[block_of(target)]
    other_side = (block_of(target) + shards_of // 2) % shards_of
    return jnp.where((block_of(source) == near) | (block_of(source) == other_side), factor * entries, entries)


def block_levels(own_key, shape, shards, least, high):
    def one(position, shards_of):
        heights = jax.random.uniform(jax.random.fold_in(jax.random.fold_in(own_key, 6), position), (shards_of,), jnp.float32, least / len(shards), high / len(shards))
        return jnp.repeat(jnp.exp(heights), shape[position] // shards_of).reshape((-1,) + (1,) * (len(shape) - position - 1))

    level = one(*shards[0])
    for cut in shards[1:]:
        level = level * one(*cut)
    return level


def gaussian(stream_key, extent, width, bound, split=(), held_as=jnp.bfloat16):
    level = block_levels(stream_key, extent, split, -0.22, 0.18) if split else 1.0
    entries = jax.random.normal(stream_key, extent, jnp.float32) * width * level
    return jnp.minimum(jnp.maximum(entries, -bound), bound).astype(held_as)


def bell_draw_with(key, shape, spread, bound, split, heavy, dtype=jnp.bfloat16):
    result = spread * jax.random.normal(key, shape, jnp.float32)
    if split:
        result = result * block_levels(key, shape, split, -0.22, 0.18)
    return jnp.clip(with_spikes(result, jax.random.fold_in(key, 3), *heavy), -bound, bound).astype(dtype)


def setup_inputs(seed: int = 0) -> dict:
    seeds = jax.random.split(jax.random.key(seed), 7)
    return {
        "tokens": bell_draw_with(seeds[0], (DOCS, L, D), 1.0, 6.0, ((1, 32),), (1, 2, 32, 2.75)),
        "cotangent": gaussian(seeds[1], (DOCS, L, D), 1.0, 6.0, ((1, 32),)),
        "conv_weight": gaussian(seeds[2], (3, D), 3 ** -0.5, 3.5, (), jnp.float32),
        "gate_weight": gaussian(seeds[3], (D, D), D ** -0.5, 0.15625, ((0, 32),)),
        "leading_block_factor": gaussian(seeds[4], (NB, BS, BS), BS ** -0.5, 0.5, ((0, 32),)),
        "trailing_block_factor": gaussian(seeds[5], (BS, NB, NB), NB ** -0.5, 0.5, ((0, 32),)),
    }


def reference(tokens, cotangent, conv_weight, gate_weight, leading_block_factor, trailing_block_factor):
    leading_wide_input = leading_block_factor.astype(jnp.float32)
    trailing_wide_input = trailing_block_factor.astype(jnp.float32)
    taps = conv_weight

    def one_doc(carry, pair):
        sum_conv, sum_gate, sum_first, sum_second = carry
        features, grad_out = pair
        feat_wide = features.astype(jnp.float32)
        pad_feat = jnp.pad(feat_wide, ((1, 1), (0, 0)))
        conv_in = (taps[0] * pad_feat[:-2] + taps[1] * feat_wide + taps[2] * pad_feat[2:]).astype(jnp.bfloat16)
        convolution_wide_input = conv_in.astype(jnp.float32).reshape(NB, BS, D)
        leading_output = jnp.einsum("shz,szy->hsy", leading_wide_input, convolution_wide_input).astype(jnp.bfloat16)
        leading_output_wide = leading_output.astype(jnp.float32)
        trailing_output = jnp.einsum("vpn,vnu->pvu", trailing_wide_input, leading_output_wide).astype(jnp.bfloat16)
        monarch = trailing_output.reshape(L, D)
        gate_act = jnp.dot(features, gate_weight, preferred_element_type=jnp.float32)
        mon_wide = monarch.astype(jnp.float32)
        grad_wide = grad_out.astype(jnp.float32)
        mixed = (mon_wide * gate_act).astype(jnp.bfloat16)
        d_monarch = (grad_wide * gate_act).astype(jnp.bfloat16)
        d_gate = (grad_wide * mon_wide).astype(jnp.bfloat16)
        second_factor_delta = d_monarch.astype(jnp.float32).reshape(NB, BS, D)
        d_first = jnp.einsum("ica,cid->aid", trailing_wide_input, second_factor_delta).astype(jnp.bfloat16)
        trailing_factor_gradient = jnp.einsum("wxn,xon->xwo", second_factor_delta, leading_output_wide)
        d_firstw = d_first.astype(jnp.float32)
        d_conv = jnp.einsum("aib,aid->abd", leading_wide_input, d_firstw).astype(jnp.bfloat16).reshape(L, D)
        grad_first = jnp.einsum("aid,abd->aib", d_firstw, convolution_wide_input)
        d_convw = d_conv.astype(jnp.float32)
        grad_conv = jnp.stack([jnp.sum(d_convw * pad_feat[:-2], axis=0), jnp.sum(d_convw * feat_wide, axis=0), jnp.sum(d_convw * pad_feat[2:], axis=0)])
        pad_grad = jnp.pad(d_convw, ((1, 1), (0, 0)))
        conv_back = taps[0] * pad_grad[2:] + taps[1] * d_convw + taps[2] * pad_grad[:-2]
        gate_back = jnp.dot(d_gate, gate_weight.T, preferred_element_type=jnp.float32)
        grad_tokens = (conv_back + gate_back).astype(jnp.bfloat16)
        grad_gate = jnp.dot(features.T, d_gate, preferred_element_type=jnp.float32)
        carry = (sum_conv + grad_conv, sum_gate + grad_gate, sum_first + grad_first, sum_second + trailing_factor_gradient)
        return carry, (mixed, grad_tokens)

    init = (jnp.zeros((3, D), jnp.float32), jnp.zeros((D, D), jnp.float32), jnp.zeros((NB, BS, BS), jnp.float32), jnp.zeros((BS, NB, NB), jnp.float32))
    carry, outs = lax.scan(one_doc, init, (tokens, cotangent))
    mixed, grad_tokens = outs
    return (mixed, grad_tokens, carry[0], carry[1], carry[2], carry[3])
```

```python
import functools

import jax
import jax.numpy as jnp
from jax import lax
from jax.experimental import pallas as pl
from jax.experimental.pallas import tpu as pltpu
from jax.sharding import PartitionSpec as P

MESH = pl.DeviceIdType.MESH
BF = jnp.bfloat16
F32 = jnp.float32
CHUNKS = 3
LIMIT = 52 * 1024 * 1024


def mm(a, b):
    return jnp.dot(a, b, preferred_element_type=F32)


def mm_t(a, b):
    return lax.dot_general(a, b, (((1,), (1,)), ((), ())), preferred_element_type=F32)


def iotas(rows, columns):
    shape = (rows, columns)
    return lax.broadcasted_iota(jnp.int32, shape, 0), lax.broadcasted_iota(jnp.int32, shape, 1)


def one_hot(mask):
    return jnp.where(mask, 1.0, 0.0).astype(BF)


def natural_order(rows, blocks, per, transposed=False):
    out, src = iotas(rows, rows)
    if transposed:
        out, src = src, out
    size = rows // blocks
    block, rest = out // size, out % size
    owner, inner = rest // per, rest % per
    return one_hot(src == owner * (blocks * per) + block * per + inner)


def inner_first(rows, per, transposed=False):
    out, src = iotas(rows, rows)
    if transposed:
        out, src = src, out
    size = rows // per
    return one_hot(src == (out % size) * per + out // size)


def greet(me, n):
    barrier = pltpu.get_barrier_semaphore()

    def body(t, carry):
        peer = lax.rem(me + t, n)
        pl.semaphore_signal(barrier, inc=1, device_id={"seq": peer}, device_id_type=MESH)
        return carry

    lax.fori_loop(1, n, body, 0)
    pl.semaphore_wait(barrier, n - 1)


def spread(me, n, k, src, dst, send_sem, recv_sem, piece):
    def body(t, carry):
        peer = lax.rem(me + lax.rem(t * 11, n), n)
        pltpu.make_async_remote_copy(
            src_ref=src.at[k, pl.ds(pl.multiple_of(peer * piece, piece), piece)],
            dst_ref=dst.at[k, pl.ds(pl.multiple_of(me * piece, piece), piece)],
            send_sem=send_sem.at[k],
            recv_sem=recv_sem.at[k],
            device_id={"seq": peer},
            device_id_type=MESH,
        ).start()
        return carry

    lax.fori_loop(1, n, body, 0)
    own = pl.ds(pl.multiple_of(me * piece, piece), piece)
    dst[k, own, :] = src[k, own, :]


def settle(ref, sem):
    pltpu.make_async_copy(ref, ref, sem).wait()


def shifted(x, before, after):
    rows = x.shape[0]
    at = lax.broadcasted_iota(jnp.int32, x.shape, 0)
    prev = jnp.where(at == 0, before, pltpu.roll(x, 1, 0))
    nxt = jnp.where(at == rows - 1, after, pltpu.roll(x, rows - 1, 0))
    return prev, nxt


def forward(
    n, tok, taps, lead, trail,
    conv, cols, mon, lead_t, trail_t, halo,
    hbuf, sa, ra, sb, rb, lead_m, trail_m, hs, hr, a_s, a_r, b_s, b_r,
):
    me = lax.axis_index("seq")
    right, left = lax.rem(me + 1, n), lax.rem(me + n - 1, n)
    rows, width = tok.shape
    blocks = lead.shape[0]
    size = lead.shape[1]
    per = size // n
    piece = blocks * per
    cw = width // CHUNKS
    greet(me, n)
    to_right = pltpu.make_async_remote_copy(
        src_ref=tok.at[pl.ds(rows - 16, 16)], dst_ref=hbuf.at[0], send_sem=hs.at[0],
        recv_sem=hr.at[0], device_id={"seq": right}, device_id_type=MESH)
    to_left = pltpu.make_async_remote_copy(
        src_ref=tok.at[pl.ds(0, 16)], dst_ref=hbuf.at[1], send_sem=hs.at[1],
        recv_sem=hr.at[1], device_id={"seq": left}, device_id_type=MESH)
    to_right.start()
    to_left.start()
    r, c = iotas(rows, rows)
    flat = jnp.concatenate([lead[a] for a in range(blocks)], axis=0)
    turned = mm(natural_order(rows, blocks, per, True), flat).astype(BF)
    wide = jnp.concatenate([turned] * blocks, axis=1)
    lead_m[...] = jnp.where((r // per) % blocks == c // size, wide, jnp.zeros_like(wide))
    to_right.wait()
    to_left.wait()
    zero = jnp.zeros((16, width), BF)
    halo[0] = jnp.where(me == 0, zero, hbuf[0])
    halo[1] = jnp.where(me == n - 1, zero, hbuf[1])
    for k in range(CHUNKS):
        at = pl.ds(k * cw, cw)
        x = tok[:, at].astype(F32)
        prev, nxt = shifted(x, halo[0, :, at].astype(F32)[15:16], halo[1, :, at].astype(F32)[0:1])
        conv[k] = (taps[0:1, at] * prev + taps[1:2, at] * x + taps[2:3, at] * nxt).astype(BF)
        sa[k] = mm(lead_m[...], conv[k]).astype(BF)
        spread(me, n, k, sa, ra, a_s, a_r, piece)
    flat = jnp.concatenate([trail[j] for j in range(per)], axis=0)
    turned = mm(inner_first(rows, per, True), flat).astype(BF)
    er, ec = iotas(size, rows)
    wide = mm(turned, one_hot(ec // per == er)).astype(BF)
    trail_m[...] = jnp.where(r % per == c % per, wide, jnp.zeros_like(wide))
    trail_t[...] = trail_m[...].T
    lead_t[...] = lead_m[...].T
    others = (n - 1) * piece
    for k in range(CHUNKS):
        settle(ra.at[k, pl.ds(0, others)], a_r.at[k])
        sb[k] = mm(trail_m[...], ra[k]).astype(BF)
        spread(me, n, k, sb, rb, b_s, b_r, piece)
        cols[k] = ra[k]
    order = natural_order(rows, blocks, per)
    for k in range(CHUNKS):
        settle(rb.at[k, pl.ds(0, others)], b_r.at[k])
        mon[k] = mm(order, rb[k]).astype(BF)
    for k in range(CHUNKS):
        settle(sa.at[k, pl.ds(0, others)], a_s.at[k])
        settle(sb.at[k, pl.ds(0, others)], b_s.at[k])


def middle(blocks, per, tok, tok_b, cot, mon, w, mixed, d_gate, send_c, part, tok_t):
    del tok_b
    rows = tok.shape[0]

    @pl.when(pl.program_id(0) == 0)
    def _():
        tok_t[...] = tok[...].T

    gate = mm(tok[...], w[...])
    m = mon[0].astype(F32)
    g = cot[...].astype(F32)
    mixed[...] = (m * gate).astype(BF)
    dg = (g * m).astype(BF)
    d_gate[...] = dg
    send_c[0] = mm(natural_order(rows, blocks, per, True), (g * gate).astype(BF)).astype(BF)
    part[...] = mm(tok_t[...], dg)


def backward(
    n, blocks, per, group, send_c, cols, trail_t, lead_t, tok, halo, conv, d_gate, w, taps,
    g_tok, g_conv, g_first, g_trail,
    rc, sd, rd, dcv, gb, hbuf, cp, p1, s2, p2, qcols,
    c_s, c_r, d_s, d_r, hs, hr, p_s, p_r, z_s, z_r,
):
    me = lax.axis_index("seq")
    right, left = lax.rem(me + 1, n), lax.rem(me + n - 1, n)
    rows, width = tok.shape
    size = rows // blocks
    piece = blocks * per
    cw = width // CHUNKS
    others = (n - 1) * piece
    teams = n // group
    mine, team = lax.rem(me, group), me // group
    greet(me, n)
    for k in range(CHUNKS):
        spread(me, n, k, send_c, rc, c_s, c_r, piece)
    swap = inner_first(rows, per)
    for k in range(CHUNKS):
        gb[k] = mm_t(d_gate[...], w[k * cw:(k + 1) * cw, :])
        qcols[k] = mm(swap, cols[k]).astype(BF)
    for k in range(CHUNKS):
        settle(rc.at[k, pl.ds(0, others)], c_r.at[k])
        sd[k] = mm(trail_t[...], rc[k]).astype(BF)
        spread(me, n, k, sd, rd, d_s, d_r, piece)
    for k in range(CHUNKS):
        turned = mm(swap, rc[k]).astype(BF)
        for j in range(per):
            at = pl.ds(j * size, size)
            term = mm_t(turned[j * size:(j + 1) * size], qcols[k, at, :])
            g_trail[j] = term if k == 0 else g_trail[j] + term
    order = natural_order(rows, blocks, per)
    for k in range(CHUNKS):
        at = pl.ds(k * cw, cw)
        settle(rd.at[k, pl.ds(0, others)], d_r.at[k])
        d = mm(lead_t[...], rd[k]).astype(BF)
        dcv[k] = d
        for side, (first, peer) in enumerate(((rows - 16, right), (0, left))):
            pltpu.make_async_remote_copy(
                src_ref=dcv.at[k, pl.ds(first, 16)], dst_ref=hbuf.at[side, k],
                send_sem=hs.at[side, k], recv_sem=hr.at[side, k],
                device_id={"seq": peer}, device_id_type=MESH).start()
        x = tok[:, at].astype(F32)
        prev, nxt = shifted(x, halo[0, :, at].astype(F32)[15:16], halo[1, :, at].astype(F32)[0:1])
        d = d.astype(F32)
        cp[k] = jnp.concatenate(
            [jnp.sum(d * v, axis=0, keepdims=True) for v in (prev, x, nxt)]
            + [jnp.zeros((5, cw), F32)], axis=0)
        p1[k, mine] = cp[k]
        for t in range(1, group):
            peer = team * group + lax.rem(mine + t, group)
            pltpu.make_async_remote_copy(
                src_ref=cp.at[k], dst_ref=p1.at[k, mine], send_sem=p_s.at[k],
                recv_sem=p_r.at[k], device_id={"seq": peer}, device_id_type=MESH).start()
        turned = mm(order, rd[k]).astype(BF)
        for a in range(blocks):
            term = mm_t(turned[a * size:(a + 1) * size], conv[k, pl.ds(a * size, size), :])
            g_first[a] = term if k == 0 else g_first[a] + term
    for k in range(CHUNKS):
        settle(p1.at[k, pl.ds(0, group - 1)], p_r.at[k])
        total = p1[k, 0]
        for t in range(1, group):
            total = total + p1[k, t]
        s2[k] = total
        p2[k, team] = total
        for t in range(1, teams):
            peer = lax.rem(me + t * group, n)
            pltpu.make_async_remote_copy(
                src_ref=s2.at[k], dst_ref=p2.at[k, team], send_sem=z_s.at[k],
                recv_sem=z_r.at[k], device_id={"seq": peer}, device_id_type=MESH).start()
    for k in range(CHUNKS):
        at = pl.ds(k * cw, cw)
        for side in range(2):
            settle(hbuf.at[side, k], hr.at[side, k])
        before = hbuf[0, k].astype(F32)[15:16]
        after = hbuf[1, k].astype(F32)[0:1]
        before = jnp.where(me == 0, jnp.zeros_like(before), before)
        after = jnp.where(me == n - 1, jnp.zeros_like(after), after)
        d = dcv[k].astype(F32)
        prev, nxt = shifted(d, before, after)
        back = taps[0:1, at] * nxt + taps[1:2, at] * d + taps[2:3, at] * prev
        g_tok[:, at] = (back + gb[k]).astype(BF)
    for k in range(CHUNKS):
        settle(p2.at[k, pl.ds(0, teams - 1)], z_r.at[k])
        total = p2[k, 0]
        for t in range(1, teams):
            total = total + p2[k, t]
        g_conv[:, pl.ds(k * cw, cw)] = total
    for k in range(CHUNKS):
        settle(send_c.at[k, pl.ds(0, others)], c_s.at[k])
        settle(sd.at[k, pl.ds(0, others)], d_s.at[k])
        settle(p1.at[k, pl.ds(0, group - 1)], p_s.at[k])
        settle(p2.at[k, pl.ds(0, teams - 1)], z_s.at[k])
        for side in range(2):
            settle(hbuf.at[side, k], hs.at[side, k])


def shards(n, tokens, cotangent, taps, gate_weight, lead, trail):
    features, grad_out = tokens[0], cotangent[0]
    rows, width = features.shape
    blocks, size = lead.shape[0], lead.shape[1]
    per = size // n
    cw = width // CHUNKS
    group = 8 if n % 8 == 0 and n > 8 else n // 2
    sds = jax.ShapeDtypeStruct
    vmem = pl.BlockSpec(memory_space=pltpu.VMEM)
    dma = pltpu.SemaphoreType.DMA
    stack = (CHUNKS, rows, cw)
    square = (rows, rows)
    block = pltpu.VMEM(stack, BF)

    whole_gate = lax.all_gather(gate_weight, "seq", axis=0, tiled=True)

    conv, cols, mon, lead_t, trail_t, halo = pl.pallas_call(
        functools.partial(forward, n),
        out_shape=[sds(stack, BF), sds(stack, BF), sds(stack, BF), sds(square, BF),
                   sds(square, BF), sds((2, 16, width), BF)],
        in_specs=[vmem] * 4,
        out_specs=[vmem] * 6,
        scratch_shapes=[pltpu.VMEM((2, 16, width), BF), block, block, block, block,
                        pltpu.VMEM(square, BF), pltpu.VMEM(square, BF), dma((2,)), dma((2,)),
                        dma((CHUNKS,)), dma((CHUNKS,)), dma((CHUNKS,)), dma((CHUNKS,))],
        compiler_params=pltpu.CompilerParams(
            collective_id=0, has_side_effects=True, vmem_limit_bytes=LIMIT),
        cost_estimate=pl.CostEstimate(
            flops=6 * rows * rows * width, bytes_accessed=200_000_000, transcendentals=0),
        name="forward_exchange",
    )(features, taps, lead, trail)

    whole_gate, mon = lax.optimization_barrier((whole_gate, mon))

    whole = pl.BlockSpec((rows, width), lambda k: (0, 0))
    strip = pl.BlockSpec((rows, cw), lambda k: (0, k))
    layer = pl.BlockSpec((1, rows, cw), lambda k: (k, 0, 0))
    tall = pl.BlockSpec((width, cw), lambda k: (0, k))
    mixed, d_gate, send_c, part = pl.pallas_call(
        functools.partial(middle, blocks, per),
        grid=(CHUNKS,),
        out_shape=[sds((rows, width), BF), sds((rows, width), BF), sds(stack, BF),
                   sds((width, width), F32)],
        in_specs=[whole, strip, strip, layer, tall],
        out_specs=[strip, strip, layer, tall],
        scratch_shapes=[pltpu.VMEM((width, rows), BF)],
        compiler_params=pltpu.CompilerParams(vmem_limit_bytes=LIMIT),
        cost_estimate=pl.CostEstimate(
            flops=4 * rows * width * width, bytes_accessed=24_000_000, transcendentals=0),
        name="gate_and_weight",
    )(features, features, grad_out, mon, whole_gate)

    part, send_c = lax.optimization_barrier((part, send_c))
    grad_gate = lax.psum_scatter(part, "seq", scatter_dimension=0, tiled=True)

    grad_tokens, grad_conv, grad_first, grad_trail = pl.pallas_call(
        functools.partial(backward, n, blocks, per, group),
        out_shape=[sds((rows, width), BF), sds((8, width), F32), sds(lead.shape, F32),
                   sds(trail.shape, F32)],
        in_specs=[vmem] * 10,
        out_specs=[vmem] * 4,
        scratch_shapes=[block, block, block, block, pltpu.VMEM(stack, F32),
                        pltpu.VMEM((2, CHUNKS, 16, cw), BF),
                        pltpu.VMEM((CHUNKS, 8, cw), F32),
                        pltpu.VMEM((CHUNKS, group, 8, cw), F32),
                        pltpu.VMEM((CHUNKS, 8, cw), F32),
                        pltpu.VMEM((CHUNKS, n // group, 8, cw), F32), block]
        + [dma((CHUNKS,))] * 4 + [dma((2, CHUNKS))] * 2 + [dma((CHUNKS,))] * 4,
        compiler_params=pltpu.CompilerParams(
            collective_id=1, has_side_effects=True, vmem_limit_bytes=LIMIT),
        cost_estimate=pl.CostEstimate(
            flops=6 * rows * rows * width, bytes_accessed=200_000_000, transcendentals=0),
        name="backward_exchange",
    )(send_c, cols, trail_t, lead_t, features, halo, conv, d_gate, whole_gate, taps)

    grad_conv, grad_gate, grad_first, grad_trail = lax.psum(
        (grad_conv[:3], grad_gate, grad_first, grad_trail), "dp")
    return mixed[None], grad_tokens[None], grad_conv, grad_gate, grad_first, grad_trail


def solution(mesh):
    seq = P("dp", "seq", None)
    specs = (seq, seq, P(), P("seq", None), P("seq", None, None), P("seq", None, None))
    return jax.shard_map(
        functools.partial(shards, mesh.shape["seq"]),
        mesh=mesh,
        in_specs=specs,
        out_specs=specs,
        check_vma=False,
    )
```

```python
import functools

import jax
import jax.numpy as jnp
from jax import lax
from jax.experimental import pallas as pl
from jax.experimental.pallas import tpu as pltpu
from jax.sharding import PartitionSpec as P

MESH = pl.DeviceIdType.MESH
BF = jnp.bfloat16
F32 = jnp.float32
CHUNKS = 2
LIMIT = 60 * 1024 * 1024


def mm(a, b):
    return jnp.dot(a, b, preferred_element_type=F32)


def mm_t(a, b):
    return lax.dot_general(a, b, (((1,), (1,)), ((), ())), preferred_element_type=F32)


def iotas(rows, columns):
    shape = (rows, columns)
    return lax.broadcasted_iota(jnp.int32, shape, 0), lax.broadcasted_iota(jnp.int32, shape, 1)


def one_hot(mask):
    return jnp.where(mask, 1.0, 0.0).astype(BF)


def natural_order(rows, blocks, per, transposed=False):
    out, src = iotas(rows, rows)
    if transposed:
        out, src = src, out
    size = rows // blocks
    block, rest = out // size, out % size
    owner, inner = rest // per, rest % per
    return one_hot(src == owner * (blocks * per) + block * per + inner)


def inner_first(rows, per, transposed=False):
    out, src = iotas(rows, rows)
    if transposed:
        out, src = src, out
    size = rows // per
    return one_hot(src == (out % size) * per + out // size)


def greet(me, n):
    barrier = pltpu.get_barrier_semaphore()

    def body(t, carry):
        peer = lax.rem(me + t, n)
        pl.semaphore_signal(barrier, inc=1, device_id={"seq": peer}, device_id_type=MESH)
        return carry

    lax.fori_loop(1, n, body, 0)
    pl.semaphore_wait(barrier, n - 1)


def spread(me, n, k, src, dst, send_sem, recv_sem, piece):
    def body(t, carry):
        peer = lax.rem(me + lax.rem(t * 11, n), n)
        pltpu.make_async_remote_copy(
            src_ref=src.at[k, pl.ds(pl.multiple_of(peer * piece, piece), piece)],
            dst_ref=dst.at[k, pl.ds(pl.multiple_of(me * piece, piece), piece)],
            send_sem=send_sem.at[k],
            recv_sem=recv_sem.at[k],
            device_id={"seq": peer},
            device_id_type=MESH,
        ).start()
        return carry

    lax.fori_loop(1, n, body, 0)
    own = pl.ds(pl.multiple_of(me * piece, piece), piece)
    dst[k, own, :] = src[k, own, :]


def settle(ref, sem):
    pltpu.make_async_copy(ref, ref, sem).wait()


def shifted(x, before, after):
    rows = x.shape[0]
    at = lax.broadcasted_iota(jnp.int32, x.shape, 0)
    prev = jnp.where(at == 0, before, pltpu.roll(x, 1, 0))
    nxt = jnp.where(at == rows - 1, after, pltpu.roll(x, rows - 1, 0))
    return prev, nxt


def flipped(me, bit):
    return me + (1 - 2 * ((me // bit) % 2)) * bit


def hop(src, dst, send_sem, recv_sem, peer):
    pltpu.make_async_remote_copy(
        src_ref=src, dst_ref=dst, send_sem=send_sem, recv_sem=recv_sem,
        device_id={"seq": peer}, device_id_type=MESH).start()


def each(count, body):
    def step(t, carry):
        body(t)
        return carry

    lax.fori_loop(0, count, step, 0)


def band(index, rows):
    return pl.ds(pl.multiple_of(index * rows, 16), rows)


ORDERS = ((2, 4), (4, 2))


def layer(
    n, tok, cot, taps, gw, lead, trail,
    mixed, g_tok, g_conv, g_gate, g_first, g_trail,
    halo, hbuf, w, part, r1, r2, r3, r4, conv, sa, ra, sb, rb, sc, rc, sd, rd, dcv, dg, gate,
    tok_t, lead_m, lead_t, trail_m, trail_t, cp, p1, s2, p2,
    a_s, a_r, b_s, b_r, c_s, c_r, d_s, d_r, t_s, t_r, hs, hr, p_s, p_r, z_s, z_r,
    w_s, w_r, g_s, g_r,
):
    me = lax.axis_index("seq")
    right, left = lax.rem(me + 1, n), lax.rem(me + n - 1, n)
    rows, width = tok.shape
    blocks, size = lead.shape[0], lead.shape[1]
    per = size // n
    piece = blocks * per
    cw = width // CHUNKS
    others = (n - 1) * piece
    own = width // n
    teams, group = n // 8, 8
    mine, team = lax.rem(me, group), me // group
    core = lax.rem(me, 2)

    def bit_of(bit):
        return (me // bit) % 2

    def gather_teams():
        for h in range(CHUNKS):
            at = pl.ds(h * cw, cw)
            w[h, band(me, own), :] = gw[:, at]
            for t in range(1, teams):
                hop(gw.at[:, at], w.at[h, band(me, own)], w_s.at[h, 0], w_r.at[h, 0],
                    lax.rem(me + t * group, n))

    def gather_step(h, stage):
        first, second = ORDERS[h]
        settle(w.at[h, pl.ds(0, (teams - 1) * own if stage == 1 else (teams << (stage - 2)) * own)],
               w_r.at[h, stage - 1])
        bit = (first, second, 1)[stage - 1]
        spans = 1 << (stage - 1)

        def body(t):
            z, v = t // spans, t % spans
            if stage == 1:
                inner = mine
            elif stage == 2:
                inner = mine - bit_of(first) * first + v * first
            else:
                inner = core + 2 * v
            d = z * group + inner
            hop(w.at[h, band(d, own)], w.at[h, band(d, own)], w_s.at[h, stage],
                w_r.at[h, stage], flipped(me, bit))

        each(teams * spans, body)

    def piece_of(h, stage, t, keep):
        first, second = ORDERS[h]
        if stage == 0:
            return 2 * t + (core if keep else 1 - core)
        mark = bit_of(first)
        if stage == 1:
            z, v = t // 2, t % 2
            return z * group + core + v * second + (mark if keep else 1 - mark) * first
        far = bit_of(second)
        return t * group + core + mark * first + (far if keep else 1 - far) * second

    landing = (r1, r2, r3)

    def scatter_step(h, stage):
        count = n >> (stage + 1)
        peer = flipped(me, (1, *ORDERS[h])[stage])

        def body(t):
            hop(part.at[h, band(piece_of(h, stage, t, False), own)],
                landing[stage].at[h, band(t, own)], g_s.at[h, stage], g_r.at[h, stage], peer)

        each(count, body)

    def scatter_sum(h, stage):
        count = n >> (stage + 1)
        settle(landing[stage].at[h], g_r.at[h, stage])

        def body(t):
            at = band(piece_of(h, stage, t, True), own)
            got = landing[stage][h, band(t, own), :].astype(F32)
            part[h, at, :] = (part[h, at, :].astype(F32) + got).astype(BF)

        each(count, body)

    def scatter_teams(h):
        r4[h, band(team, own), :] = part[h, band(me, own), :]
        for t in range(1, teams):
            peer = lax.rem(me + t * group, n)
            hop(part.at[h, band(peer, own)], r4.at[h, band(team, own)], g_s.at[h, 3],
                g_r.at[h, 3], peer)

    greet(me, n)
    hop(tok.at[pl.ds(rows - 16, 16)], halo.at[0], t_s.at[0], t_r.at[0], right)
    hop(tok.at[pl.ds(0, 16)], halo.at[1], t_s.at[1], t_r.at[1], left)
    gather_teams()
    r, c = iotas(rows, rows)
    flat = jnp.concatenate([lead[a] for a in range(blocks)], axis=0)
    turned = mm(natural_order(rows, blocks, per, True), flat).astype(BF)
    wide = jnp.concatenate([turned] * blocks, axis=1)
    lead_m[...] = jnp.where((r // per) % blocks == c // size, wide, jnp.zeros_like(wide))
    for side in range(2):
        settle(halo.at[side], t_r.at[side])

    def around(k):
        at = pl.ds(k * cw, cw)
        x = tok[:, at].astype(F32)
        before = halo[0, :, at].astype(F32)[15:16]
        after = halo[1, :, at].astype(F32)[0:1]
        before = jnp.where(me == 0, jnp.zeros_like(before), before)
        after = jnp.where(me == n - 1, jnp.zeros_like(after), after)
        prev, nxt = shifted(x, before, after)
        return prev, x, nxt

    for k in range(CHUNKS):
        at = pl.ds(k * cw, cw)
        prev, x, nxt = around(k)
        conv[k] = (taps[0:1, at] * prev + taps[1:2, at] * x + taps[2:3, at] * nxt).astype(BF)
        sa[k] = mm(lead_m[...], conv[k]).astype(BF)
        spread(me, n, k, sa, ra, a_s, a_r, piece)
    flat = jnp.concatenate([trail[j] for j in range(per)], axis=0)
    turned = mm(inner_first(rows, per, True), flat).astype(BF)
    er, ec = iotas(size, rows)
    wide = mm(turned, one_hot(ec // per == er)).astype(BF)
    trail_m[...] = jnp.where(r % per == c % per, wide, jnp.zeros_like(wide))
    for h in range(CHUNKS):
        gather_step(h, 1)
    trail_t[...] = trail_m[...].T
    lead_t[...] = lead_m[...].T
    tok_t[...] = tok[...].T
    for h in range(CHUNKS):
        gather_step(h, 2)
    for k in range(CHUNKS):
        settle(ra.at[k, pl.ds(0, others)], a_r.at[k])
        sb[k] = mm(trail_m[...], ra[k]).astype(BF)
        spread(me, n, k, sb, rb, b_s, b_r, piece)
        gather_step(k, 3)
    order_t = natural_order(rows, blocks, per, True)
    for k in range(CHUNKS):
        at = pl.ds(k * cw, cw)
        settle(w.at[k, pl.ds(0, n // 2 * own)], w_r.at[k, 3])
        gate[k] = mm(tok[...], w[k])
        d_mon = (cot[:, at].astype(F32) * gate[k]).astype(BF)
        sc[k] = mm(order_t, d_mon).astype(BF)
        spread(me, n, k, sc, rc, c_s, c_r, piece)
    order = natural_order(rows, blocks, per)
    strip = width // 4
    for k in range(CHUNKS):
        at = pl.ds(k * cw, cw)
        settle(rb.at[k, pl.ds(0, others)], b_r.at[k])
        m = mm(order, rb[k]).astype(BF).astype(F32)
        mixed[:, at] = (m * gate[k]).astype(BF)
        dg[k] = (cot[:, at].astype(F32) * m).astype(BF)
        for q in range(4):
            part[k, q * strip:(q + 1) * strip, :] = mm(
                tok_t[q * strip:(q + 1) * strip, :], dg[k]).astype(BF)
        scatter_step(k, 0)
    swap = inner_first(rows, per)
    for k in range(CHUNKS):
        rb[k] = mm(swap, ra[k]).astype(BF)
    for k in range(CHUNKS):
        scatter_sum(k, 0)
        scatter_step(k, 1)
    for k in range(CHUNKS):
        settle(rc.at[k, pl.ds(0, others)], c_r.at[k])
        sd[k] = mm(trail_t[...], rc[k]).astype(BF)
        spread(me, n, k, sd, rd, d_s, d_r, piece)
    for k in range(CHUNKS):
        back = mm_t(dg[0], w[0, k * cw:(k + 1) * cw, :])
        for h in range(1, CHUNKS):
            back = back + mm_t(dg[h], w[h, k * cw:(k + 1) * cw, :])
        gate[k] = back
    for k in range(CHUNKS):
        scatter_sum(k, 1)
        scatter_step(k, 2)
    for k in range(CHUNKS):
        turned = mm(swap, rc[k]).astype(BF)
        for j in range(per):
            term = mm_t(turned[j * size:(j + 1) * size], rb[k, pl.ds(j * size, size), :])
            g_trail[j] = term if k == 0 else g_trail[j] + term
    for k in range(CHUNKS):
        scatter_sum(k, 2)
        scatter_teams(k)
    for k in range(CHUNKS):
        settle(rd.at[k, pl.ds(0, others)], d_r.at[k])
        d = mm(lead_t[...], rd[k]).astype(BF)
        dcv[k] = d
        hop(dcv.at[k, pl.ds(rows - 16, 16)], hbuf.at[0, k], hs.at[0, k], hr.at[0, k], right)
        hop(dcv.at[k, pl.ds(0, 16)], hbuf.at[1, k], hs.at[1, k], hr.at[1, k], left)
        d = d.astype(F32)
        cp[k] = jnp.concatenate(
            [jnp.sum(d * v, axis=0, keepdims=True) for v in around(k)]
            + [jnp.zeros((5, cw), F32)], axis=0)
        p1[k, mine] = cp[k]
        for t in range(1, group):
            hop(cp.at[k], p1.at[k, mine], p_s.at[k], p_r.at[k],
                team * group + lax.rem(mine + t, group))
        turned = mm(order, rd[k]).astype(BF)
        for a in range(blocks):
            term = mm_t(turned[a * size:(a + 1) * size], conv[k, pl.ds(a * size, size), :])
            g_first[a] = term if k == 0 else g_first[a] + term
    for k in range(CHUNKS):
        settle(p1.at[k, pl.ds(0, group - 1)], p_r.at[k])
        total = p1[k, 0]
        for t in range(1, group):
            total = total + p1[k, t]
        s2[k] = total
        p2[k, team] = total
        for t in range(1, teams):
            hop(s2.at[k], p2.at[k, team], z_s.at[k], z_r.at[k], lax.rem(me + t * group, n))
    for k in range(CHUNKS):
        at = pl.ds(k * cw, cw)
        for side in range(2):
            settle(hbuf.at[side, k], hr.at[side, k])
        before = hbuf[0, k].astype(F32)[15:16]
        after = hbuf[1, k].astype(F32)[0:1]
        before = jnp.where(me == 0, jnp.zeros_like(before), before)
        after = jnp.where(me == n - 1, jnp.zeros_like(after), after)
        d = dcv[k].astype(F32)
        prev, nxt = shifted(d, before, after)
        back = taps[0:1, at] * nxt + taps[1:2, at] * d + taps[2:3, at] * prev
        g_tok[:, at] = (back + gate[k]).astype(BF)
    for k in range(CHUNKS):
        at = pl.ds(k * cw, cw)
        settle(r4.at[k, pl.ds(0, (teams - 1) * own)], g_r.at[k, 3])
        total = r4[k, pl.ds(0, own), :].astype(F32)
        for t in range(1, teams):
            total = total + r4[k, pl.ds(t * own, own), :].astype(F32)
        g_gate[:, at] = total
        settle(p2.at[k, pl.ds(0, teams - 1)], z_r.at[k])
        total = p2[k, 0]
        for t in range(1, teams):
            total = total + p2[k, t]
        g_conv[:, at] = total
    for k in range(CHUNKS):
        settle(halo.at[k], t_s.at[k])
        for buf, sem in ((sa, a_s), (sb, b_s), (sc, c_s), (sd, d_s)):
            settle(buf.at[k, pl.ds(0, others)], sem.at[k])
        for stage in range(4):
            count = (teams - 1) if stage == 0 else teams << (stage - 1)
            settle(w.at[k, pl.ds(0, count * own)], w_s.at[k, stage])
            count = (teams - 1) if stage == 3 else n >> (stage + 1)
            settle(part.at[k, pl.ds(0, count * own)], g_s.at[k, stage])
        settle(p1.at[k, pl.ds(0, group - 1)], p_s.at[k])
        settle(p2.at[k, pl.ds(0, teams - 1)], z_s.at[k])
        for side in range(2):
            settle(hbuf.at[side, k], hs.at[side, k])


def shards(n, tokens, cotangent, taps, gate_weight, lead, trail):
    features, grad_out = tokens[0], cotangent[0]
    rows, width = features.shape
    cw = width // CHUNKS
    own = width // n
    sds = jax.ShapeDtypeStruct
    vmem = pl.BlockSpec(memory_space=pltpu.VMEM)
    dma = pltpu.SemaphoreType.DMA
    block = pltpu.VMEM((CHUNKS, rows, cw), BF)
    square = pltpu.VMEM((rows, rows), BF)
    whole = pltpu.VMEM((CHUNKS, width, cw), BF)

    def pieces(count):
        return pltpu.VMEM((CHUNKS, count * own, cw), BF)

    def tails(count):
        return pltpu.VMEM((CHUNKS, count, 8, cw), F32)

    mixed, grad_tokens, grad_conv, grad_gate, grad_first, grad_trail = pl.pallas_call(
        functools.partial(layer, n),
        out_shape=[sds((rows, width), BF), sds((rows, width), BF), sds((8, width), F32),
                   sds((own, width), F32), sds(lead.shape, F32), sds(trail.shape, F32)],
        in_specs=[vmem] * 6,
        out_specs=[vmem] * 6,
        scratch_shapes=[pltpu.VMEM((2, 16, width), BF), pltpu.VMEM((2, CHUNKS, 16, cw), BF),
                        whole, whole, pieces(n // 2), pieces(n // 4), pieces(n // 8),
                        pieces(n // 8)]
        + [block] * 11
        + [pltpu.VMEM((CHUNKS, rows, cw), F32), pltpu.VMEM((width, rows), BF)]
        + [square] * 4
        + [pltpu.VMEM((CHUNKS, 8, cw), F32), tails(8), pltpu.VMEM((CHUNKS, 8, cw), F32),
           tails(n // 8)]
        + [dma((CHUNKS,))] * 8 + [dma((2,))] * 2 + [dma((2, CHUNKS))] * 2
        + [dma((CHUNKS,))] * 4 + [dma((CHUNKS, 4))] * 4,
        compiler_params=pltpu.CompilerParams(
            collective_id=0, has_side_effects=True, vmem_limit_bytes=LIMIT),
        cost_estimate=pl.CostEstimate(
            flops=12 * rows * width * width, bytes_accessed=10_000_000, transcendentals=0),
        name="layer",
    )(features, grad_out, taps, gate_weight, lead, trail)

    grad_conv, grad_gate, grad_first, grad_trail = lax.psum(
        (grad_conv[:3], grad_gate, grad_first, grad_trail), "dp")
    return mixed[None], grad_tokens[None], grad_conv, grad_gate, grad_first, grad_trail


def solution(mesh):
    seq = P("dp", "seq", None)
    specs = (seq, seq, P(), P("seq", None), P("seq", None, None), P("seq", None, None))
    return jax.shard_map(
        functools.partial(shards, mesh.shape["seq"]),
        mesh=mesh,
        in_specs=specs,
        out_specs=specs,
        check_vma=False,
    )
```

```python
import functools

import jax
import jax.numpy as jnp
from jax import lax
from jax.experimental import pallas as pl
from jax.experimental.pallas import tpu as pltpu
from jax.sharding import PartitionSpec as P

MESH = pl.DeviceIdType.MESH
BF = jnp.bfloat16
F32 = jnp.float32
CHUNKS = 2
LIMIT = 60 * 1024 * 1024


def mm(a, b):
    return jnp.dot(a, b, preferred_element_type=F32)


def mm_t(a, b):
    return lax.dot_general(a, b, (((1,), (1,)), ((), ())), preferred_element_type=F32)


def iotas(rows, columns):
    shape = (rows, columns)
    return lax.broadcasted_iota(jnp.int32, shape, 0), lax.broadcasted_iota(jnp.int32, shape, 1)


def one_hot(mask):
    return jnp.where(mask, 1.0, 0.0).astype(BF)


def natural_order(rows, blocks, per, transposed=False):
    out, src = iotas(rows, rows)
    if transposed:
        out, src = src, out
    size = rows // blocks
    block, rest = out // size, out % size
    owner, inner = rest // per, rest % per
    return one_hot(src == owner * (blocks * per) + block * per + inner)


def inner_first(rows, per, transposed=False):
    out, src = iotas(rows, rows)
    if transposed:
        out, src = src, out
    size = rows // per
    return one_hot(src == (out % size) * per + out // size)


def greet(me, n):
    barrier = pltpu.get_barrier_semaphore()

    def body(t, carry):
        peer = lax.rem(me + t, n)
        pl.semaphore_signal(barrier, inc=1, device_id={"seq": peer}, device_id_type=MESH)
        return carry

    lax.fori_loop(1, n, body, 0)
    return barrier


def spread(me, n, k, src, dst, send_sem, recv_sem, piece):
    def body(t, carry):
        peer = lax.rem(me + lax.rem(t * 11, n), n)
        pltpu.make_async_remote_copy(
            src_ref=src.at[k, pl.ds(pl.multiple_of(peer * piece, piece), piece)],
            dst_ref=dst.at[k, pl.ds(pl.multiple_of(me * piece, piece), piece)],
            send_sem=send_sem.at[k],
            recv_sem=recv_sem.at[k],
            device_id={"seq": peer},
            device_id_type=MESH,
        ).start()
        return carry

    lax.fori_loop(1, n, body, 0)
    own = pl.ds(pl.multiple_of(me * piece, piece), piece)
    dst[k, own, :] = src[k, own, :]


def settle(ref, sem):
    pltpu.make_async_copy(ref, ref, sem).wait()


def shifted(x, before, after):
    rows = x.shape[0]
    at = lax.broadcasted_iota(jnp.int32, x.shape, 0)
    prev = jnp.where(at == 0, before, pltpu.roll(x, 1, 0))
    nxt = jnp.where(at == rows - 1, after, pltpu.roll(x, rows - 1, 0))
    return prev, nxt


def flipped(me, bit):
    return me + (1 - 2 * ((me // bit) % 2)) * bit


def hop(src, dst, send_sem, recv_sem, peer):
    pltpu.make_async_remote_copy(
        src_ref=src, dst_ref=dst, send_sem=send_sem, recv_sem=recv_sem,
        device_id={"seq": peer}, device_id_type=MESH).start()


def each(count, body):
    def step(t, carry):
        body(t)
        return carry

    lax.fori_loop(0, count, step, 0)


def band(index, rows):
    return pl.ds(pl.multiple_of(index * rows, 16), rows)


ORDERS = ((2, 4), (4, 2))


def layer(
    n, tok, cot_in, taps, gw, lead, trail,
    mixed_out, g_tok_out, g_conv, g_gate, g_first, g_trail,
    cot, mixed, g_tok, halo, hbuf, w, part, r1, r2, r3, r4, conv, sa, ra, sb, rb, sc, rc, sd, rd, dcv, dg, gate,
    tok_t, lead_m, lead_t, trail_m, trail_t, cp, p1, s2, p2,
    a_s, a_r, b_s, b_r, c_s, c_r, d_s, d_r, t_s, t_r, hs, hr, p_s, p_r, z_s, z_r,
    w_s, w_r, g_s, g_r, in_s, m_s, o_s,
):
    me = lax.axis_index("seq")
    right, left = lax.rem(me + 1, n), lax.rem(me + n - 1, n)
    rows, width = tok.shape
    blocks, size = lead.shape[0], lead.shape[1]
    per = size // n
    piece = blocks * per
    cw = width // CHUNKS
    others = (n - 1) * piece
    own = width // n
    teams, group = n // 8, 8
    mine, team = lax.rem(me, group), me // group
    core = lax.rem(me, 2)

    def bit_of(bit):
        return (me // bit) % 2

    def gather_teams():
        for h in range(CHUNKS):
            at = pl.ds(h * cw, cw)
            w[h, band(me, own), :] = gw[:, at]
            for t in range(1, teams):
                hop(gw.at[:, at], w.at[h, band(me, own)], w_s.at[h, 0], w_r.at[h, 0],
                    lax.rem(me + t * group, n))

    def gather_step(h, stage):
        first, second = ORDERS[h]
        settle(w.at[h, pl.ds(0, (teams - 1) * own if stage == 1 else (teams << (stage - 2)) * own)],
               w_r.at[h, stage - 1])
        bit = (first, second, 1)[stage - 1]
        spans = 1 << (stage - 1)

        def body(t):
            z, v = t // spans, t % spans
            if stage == 1:
                inner = mine
            elif stage == 2:
                inner = mine - bit_of(first) * first + v * first
            else:
                inner = core + 2 * v
            d = z * group + inner
            hop(w.at[h, band(d, own)], w.at[h, band(d, own)], w_s.at[h, stage],
                w_r.at[h, stage], flipped(me, bit))

        each(teams * spans, body)

    def piece_of(h, stage, t, keep):
        first, second = ORDERS[h]
        if stage == 0:
            return 2 * t + (core if keep else 1 - core)
        mark = bit_of(first)
        if stage == 1:
            z, v = t // 2, t % 2
            return z * group + core + v * second + (mark if keep else 1 - mark) * first
        far = bit_of(second)
        return t * group + core + mark * first + (far if keep else 1 - far) * second

    landing = (r1, r2, r3)

    def scatter_step(h, stage):
        count = n >> (stage + 1)
        peer = flipped(me, (1, *ORDERS[h])[stage])

        def body(t):
            hop(part.at[h, band(piece_of(h, stage, t, False), own)],
                landing[stage].at[h, band(t, own)], g_s.at[h, stage], g_r.at[h, stage], peer)

        each(count, body)

    def scatter_sum(h, stage):
        count = n >> (stage + 1)
        settle(landing[stage].at[h], g_r.at[h, stage])

        def body(t):
            at = band(piece_of(h, stage, t, True), own)
            got = landing[stage][h, band(t, own), :].astype(F32)
            part[h, at, :] = (part[h, at, :].astype(F32) + got).astype(BF)

        each(count, body)

    def scatter_teams(h):
        r4[h, band(team, own), :] = part[h, band(me, own), :]
        for t in range(1, teams):
            peer = lax.rem(me + t * group, n)
            hop(part.at[h, band(peer, own)], r4.at[h, band(team, own)], g_s.at[h, 3],
                g_r.at[h, 3], peer)

    def leaving(src, dst, k, sem):
        at = pl.ds(k * cw, cw)
        return pltpu.make_async_copy(src.at[:, at], dst.at[:, at], sem.at[k])

    barrier = greet(me, n)
    fetch = pltpu.make_async_copy(cot_in, cot, in_s.at[0])
    fetch.start()
    r, c = iotas(rows, rows)
    flat = jnp.concatenate([lead[a] for a in range(blocks)], axis=0)
    turned = mm(natural_order(rows, blocks, per, True), flat).astype(BF)
    wide = jnp.concatenate([turned] * blocks, axis=1)
    lead_m[...] = jnp.where((r // per) % blocks == c // size, wide, jnp.zeros_like(wide))

    def taps_over(at, prev, x, nxt):
        return (taps[0:1, at] * prev + taps[1:2, at] * x + taps[2:3, at] * nxt).astype(BF)

    for k in range(CHUNKS):
        at = pl.ds(k * cw, cw)
        x = tok[:, at].astype(F32)
        none = jnp.zeros((1, cw), F32)
        prev, nxt = shifted(x, none, none)
        conv[k] = taps_over(at, prev, x, nxt)
    pl.semaphore_wait(barrier, n - 1)
    hop(tok.at[pl.ds(rows - 16, 16)], halo.at[0], t_s.at[0], t_r.at[0], right)
    hop(tok.at[pl.ds(0, 16)], halo.at[1], t_s.at[1], t_r.at[1], left)
    gather_teams()
    for side in range(2):
        settle(halo.at[side], t_r.at[side])

    def sides(k):
        at = pl.ds(k * cw, cw)
        before = halo[0, :, at].astype(F32)[15:16]
        after = halo[1, :, at].astype(F32)[0:1]
        before = jnp.where(me == 0, jnp.zeros_like(before), before)
        after = jnp.where(me == n - 1, jnp.zeros_like(after), after)
        return before, after

    def around(k):
        at = pl.ds(k * cw, cw)
        x = tok[:, at].astype(F32)
        prev, nxt = shifted(x, *sides(k))
        return prev, x, nxt

    for k in range(CHUNKS):
        at = pl.ds(k * cw, cw)
        edge = lax.broadcasted_iota(jnp.int32, (16, cw), 0)
        for first, row in ((0, 0), (rows - 16, 15)):
            slab = pl.ds(first, 16)
            x = tok[slab, at].astype(F32)
            prev, nxt = shifted(x, *sides(k))
            fixed = taps_over(at, prev, x, nxt).astype(F32)
            conv[k, slab, :] = jnp.where(edge == row, fixed, conv[k, slab, :].astype(F32)).astype(BF)
        sa[k] = mm(lead_m[...], conv[k]).astype(BF)
        spread(me, n, k, sa, ra, a_s, a_r, piece)
    flat = jnp.concatenate([trail[j] for j in range(per)], axis=0)
    turned = mm(inner_first(rows, per, True), flat).astype(BF)
    er, ec = iotas(size, rows)
    wide = mm(turned, one_hot(ec // per == er)).astype(BF)
    trail_m[...] = jnp.where(r % per == c % per, wide, jnp.zeros_like(wide))
    for h in range(CHUNKS):
        gather_step(h, 1)
    trail_t[...] = trail_m[...].T
    lead_t[...] = lead_m[...].T
    tok_t[...] = tok[...].T
    for h in range(CHUNKS):
        gather_step(h, 2)
    for k in range(CHUNKS):
        settle(ra.at[k, pl.ds(0, others)], a_r.at[k])
        sb[k] = mm(trail_m[...], ra[k]).astype(BF)
        spread(me, n, k, sb, rb, b_s, b_r, piece)
        gather_step(k, 3)
    order_t = natural_order(rows, blocks, per, True)
    fetch.wait()
    for k in range(CHUNKS):
        at = pl.ds(k * cw, cw)
        settle(w.at[k, pl.ds(0, n // 2 * own)], w_r.at[k, 3])
        gate[k] = mm(tok[...], w[k])
        d_mon = (cot[:, at].astype(F32) * gate[k]).astype(BF)
        sc[k] = mm(order_t, d_mon).astype(BF)
        spread(me, n, k, sc, rc, c_s, c_r, piece)
    order = natural_order(rows, blocks, per)
    strip = width // 4
    for k in range(CHUNKS):
        at = pl.ds(k * cw, cw)
        settle(rb.at[k, pl.ds(0, others)], b_r.at[k])
        m = mm(order, rb[k]).astype(BF).astype(F32)
        mixed[:, at] = (m * gate[k]).astype(BF)
        leaving(mixed, mixed_out, k, m_s).start()
        dg[k] = (cot[:, at].astype(F32) * m).astype(BF)
        for q in range(4):
            part[k, q * strip:(q + 1) * strip, :] = mm(
                tok_t[q * strip:(q + 1) * strip, :], dg[k]).astype(BF)
        scatter_step(k, 0)
    swap = inner_first(rows, per)
    for k in range(CHUNKS):
        rb[k] = mm(swap, ra[k]).astype(BF)
    for k in range(CHUNKS):
        settle(rc.at[k, pl.ds(0, others)], c_r.at[k])
        sd[k] = mm(trail_t[...], rc[k]).astype(BF)
        spread(me, n, k, sd, rd, d_s, d_r, piece)
        if k == 0:
            for h in range(CHUNKS):
                scatter_sum(h, 0)
                scatter_step(h, 1)
    for k in range(CHUNKS):
        back = mm_t(dg[0], w[0, k * cw:(k + 1) * cw, :])
        for h in range(1, CHUNKS):
            back = back + mm_t(dg[h], w[h, k * cw:(k + 1) * cw, :])
        gate[k] = back
    for k in range(CHUNKS):
        scatter_sum(k, 1)
        scatter_step(k, 2)
    for k in range(CHUNKS):
        turned = mm(swap, rc[k]).astype(BF)
        for j in range(per):
            term = mm_t(turned[j * size:(j + 1) * size], rb[k, pl.ds(j * size, size), :])
            g_trail[j] = term if k == 0 else g_trail[j] + term
    for k in range(CHUNKS):
        scatter_sum(k, 2)
        scatter_teams(k)
    for k in range(CHUNKS):
        settle(rd.at[k, pl.ds(0, others)], d_r.at[k])
        d = mm(lead_t[...], rd[k]).astype(BF)
        dcv[k] = d
        hop(dcv.at[k, pl.ds(rows - 16, 16)], hbuf.at[0, k], hs.at[0, k], hr.at[0, k], right)
        hop(dcv.at[k, pl.ds(0, 16)], hbuf.at[1, k], hs.at[1, k], hr.at[1, k], left)
        d = d.astype(F32)
        cp[k] = jnp.concatenate(
            [jnp.sum(d * v, axis=0, keepdims=True) for v in around(k)]
            + [jnp.zeros((5, cw), F32)], axis=0)
        p1[k, mine] = cp[k]
        for t in range(1, group):
            hop(cp.at[k], p1.at[k, mine], p_s.at[k], p_r.at[k],
                team * group + lax.rem(mine + t, group))
        turned = mm(order, rd[k]).astype(BF)
        for a in range(blocks):
            term = mm_t(turned[a * size:(a + 1) * size], conv[k, pl.ds(a * size, size), :])
            g_first[a] = term if k == 0 else g_first[a] + term
    for k in range(CHUNKS):
        settle(p1.at[k, pl.ds(0, group - 1)], p_r.at[k])
        total = p1[k, 0]
        for t in range(1, group):
            total = total + p1[k, t]
        s2[k] = total
        p2[k, team] = total
        for t in range(1, teams):
            hop(s2.at[k], p2.at[k, team], z_s.at[k], z_r.at[k], lax.rem(me + t * group, n))
    for k in range(CHUNKS):
        at = pl.ds(k * cw, cw)
        for side in range(2):
            settle(hbuf.at[side, k], hr.at[side, k])
        before = hbuf[0, k].astype(F32)[15:16]
        after = hbuf[1, k].astype(F32)[0:1]
        before = jnp.where(me == 0, jnp.zeros_like(before), before)
        after = jnp.where(me == n - 1, jnp.zeros_like(after), after)
        d = dcv[k].astype(F32)
        prev, nxt = shifted(d, before, after)
        back = taps[0:1, at] * nxt + taps[1:2, at] * d + taps[2:3, at] * prev
        g_tok[:, at] = (back + gate[k]).astype(BF)
        leaving(g_tok, g_tok_out, k, o_s).start()
    for k in range(CHUNKS):
        at = pl.ds(k * cw, cw)
        settle(r4.at[k, pl.ds(0, (teams - 1) * own)], g_r.at[k, 3])
        total = r4[k, pl.ds(0, own), :].astype(F32)
        for t in range(1, teams):
            total = total + r4[k, pl.ds(t * own, own), :].astype(F32)
        g_gate[:, at] = total
        settle(p2.at[k, pl.ds(0, teams - 1)], z_r.at[k])
        total = p2[k, 0]
        for t in range(1, teams):
            total = total + p2[k, t]
        g_conv[:, at] = total[0:3]
    for side in range(2):
        settle(halo.at[side], t_s.at[side])
    for k in range(CHUNKS):
        leaving(mixed, mixed_out, k, m_s).wait()
        leaving(g_tok, g_tok_out, k, o_s).wait()
        for buf, sem in ((sa, a_s), (sb, b_s), (sc, c_s), (sd, d_s)):
            settle(buf.at[k, pl.ds(0, others)], sem.at[k])
        for stage in range(4):
            count = (teams - 1) if stage == 0 else teams << (stage - 1)
            settle(w.at[k, pl.ds(0, count * own)], w_s.at[k, stage])
            count = (teams - 1) if stage == 3 else n >> (stage + 1)
            settle(part.at[k, pl.ds(0, count * own)], g_s.at[k, stage])
        settle(p1.at[k, pl.ds(0, group - 1)], p_s.at[k])
        settle(p2.at[k, pl.ds(0, teams - 1)], z_s.at[k])
        for side in range(2):
            settle(hbuf.at[side, k], hs.at[side, k])


CUTS = (4, 4, 1, 1, 1, 1)


def handed_on(*refs):
    count = len(CUTS)
    srcs, dsts, sem = refs[:count], refs[count:2 * count], refs[-1]
    copies = []
    for cuts, src, dst in zip(CUTS, srcs, dsts):
        step = src.shape[0] // cuts
        for q in range(cuts):
            at = pl.ds(q * step, step)
            copies.append(pltpu.make_async_copy(src.at[at], dst.at[at], sem.at[len(copies)]))
    for copy in copies:
        copy.start()
    for copy in copies:
        copy.wait()


def shards(n, tokens, cotangent, taps, gate_weight, lead, trail):
    features, grad_out = tokens[0], cotangent[0]
    rows, width = features.shape
    cw = width // CHUNKS
    own = width // n
    sds = jax.ShapeDtypeStruct
    vmem = pl.BlockSpec(memory_space=pltpu.VMEM)
    dma = pltpu.SemaphoreType.DMA
    block = pltpu.VMEM((CHUNKS, rows, cw), BF)
    square = pltpu.VMEM((rows, rows), BF)
    whole = pltpu.VMEM((CHUNKS, width, cw), BF)

    def pieces(count):
        return pltpu.VMEM((CHUNKS, count * own, cw), BF)

    def tails(count):
        return pltpu.VMEM((CHUNKS, count, 8, cw), F32)

    anywhere = pl.BlockSpec(memory_space=pl.ANY)
    shapes = [sds((rows, width), BF), sds((rows, width), BF), sds((3, width), F32),
              sds((own, width), F32), sds(lead.shape, F32), sds(trail.shape, F32)]
    results = pl.pallas_call(
        functools.partial(layer, n),
        out_shape=shapes,
        in_specs=[vmem, anywhere] + [vmem] * 4,
        out_specs=[anywhere] * 2 + [vmem] * 4,
        scratch_shapes=[pltpu.VMEM((rows, width), BF)] * 3 + [pltpu.VMEM((2, 16, width), BF), pltpu.VMEM((2, CHUNKS, 16, cw), BF),
                        whole, whole, pieces(n // 2), pieces(n // 4), pieces(n // 8),
                        pieces(n // 8)]
        + [block] * 11
        + [pltpu.VMEM((CHUNKS, rows, cw), F32), pltpu.VMEM((width, rows), BF)]
        + [square] * 4
        + [pltpu.VMEM((CHUNKS, 8, cw), F32), tails(8), pltpu.VMEM((CHUNKS, 8, cw), F32),
           tails(n // 8)]
        + [dma((CHUNKS,))] * 8 + [dma((2,))] * 2 + [dma((2, CHUNKS))] * 2
        + [dma((CHUNKS,))] * 4 + [dma((CHUNKS, 4))] * 4 + [dma((1,)), dma((CHUNKS,)), dma((CHUNKS,))],
        compiler_params=pltpu.CompilerParams(
            collective_id=0, has_side_effects=True, vmem_limit_bytes=LIMIT),
        cost_estimate=pl.CostEstimate(
            flops=12 * rows * width * width, bytes_accessed=10_000_000, transcendentals=0),
        name="layer",
    )(features, grad_out, taps, gate_weight, lead, trail)

    mixed, grad_tokens, grad_conv, grad_gate, grad_first, grad_trail = pl.pallas_call(
        handed_on,
        out_shape=shapes,
        in_specs=[anywhere] * 6,
        out_specs=[anywhere] * 6,
        scratch_shapes=[dma((sum(CUTS),))],
        compiler_params=pltpu.CompilerParams(vmem_limit_bytes=LIMIT),
        name="handed_on",
    )(*results)

    grad_conv, grad_gate, grad_first, grad_trail = lax.psum(
        (grad_conv, grad_gate, grad_first, grad_trail), "dp")
    return mixed[None], grad_tokens[None], grad_conv, grad_gate, grad_first, grad_trail


def solution(mesh):
    seq = P("dp", "seq", None)
    specs = (seq, seq, P(), P("seq", None), P("seq", None, None), P("seq", None, None))
    return jax.shard_map(
        functools.partial(shards, mesh.shape["seq"]),
        mesh=mesh,
        in_specs=specs,
        out_specs=specs,
        check_vma=False,
    )
```

```python
import functools

import jax
import jax.numpy as jnp
from jax import lax
from jax.experimental import pallas as pl
from jax.experimental.pallas import tpu as pltpu
from jax.sharding import PartitionSpec as P

MESH = pl.DeviceIdType.MESH
BF = jnp.bfloat16
F32 = jnp.float32
CHUNKS = 2
LIMIT = 60 * 1024 * 1024


def mm(a, b):
    return jnp.dot(a, b, preferred_element_type=F32)


def mm_t(a, b):
    return lax.dot_general(a, b, (((1,), (1,)), ((), ())), preferred_element_type=F32)


def iotas(rows, columns):
    shape = (rows, columns)
    return lax.broadcasted_iota(jnp.int32, shape, 0), lax.broadcasted_iota(jnp.int32, shape, 1)


def one_hot(mask):
    return jnp.where(mask, 1.0, 0.0).astype(BF)


def natural_order(rows, blocks, per, transposed=False):
    out, src = iotas(rows, rows)
    if transposed:
        out, src = src, out
    size = rows // blocks
    block, rest = out // size, out % size
    owner, inner = rest // per, rest % per
    return one_hot(src == owner * (blocks * per) + block * per + inner)


def inner_first(rows, per, transposed=False):
    out, src = iotas(rows, rows)
    if transposed:
        out, src = src, out
    size = rows // per
    return one_hot(src == (out % size) * per + out // size)


def greet(me, n):
    barrier = pltpu.get_barrier_semaphore()

    def body(t, carry):
        peer = lax.rem(me + t, n)
        pl.semaphore_signal(barrier, inc=1, device_id={"seq": peer}, device_id_type=MESH)
        return carry

    lax.fori_loop(1, n, body, 0)
    return barrier


def spread(me, n, k, src, dst, send_sem, recv_sem, piece):
    def body(t, carry):
        peer = lax.rem(me + lax.rem(t * 11, n), n)
        pltpu.make_async_remote_copy(
            src_ref=src.at[k, pl.ds(pl.multiple_of(peer * piece, piece), piece)],
            dst_ref=dst.at[k, pl.ds(pl.multiple_of(me * piece, piece), piece)],
            send_sem=send_sem.at[k],
            recv_sem=recv_sem.at[k],
            device_id={"seq": peer},
            device_id_type=MESH,
        ).start()
        return carry

    lax.fori_loop(1, n, body, 0)
    own = pl.ds(pl.multiple_of(me * piece, piece), piece)
    dst[k, own, :] = src[k, own, :]


def settle(ref, sem):
    pltpu.make_async_copy(ref, ref, sem).wait()


def shifted(x, before, after):
    rows = x.shape[0]
    at = lax.broadcasted_iota(jnp.int32, x.shape, 0)
    prev = jnp.where(at == 0, before, pltpu.roll(x, 1, 0))
    nxt = jnp.where(at == rows - 1, after, pltpu.roll(x, rows - 1, 0))
    return prev, nxt


def flipped(me, bit):
    return me + (1 - 2 * ((me // bit) % 2)) * bit


def hop(src, dst, send_sem, recv_sem, peer):
    pltpu.make_async_remote_copy(
        src_ref=src, dst_ref=dst, send_sem=send_sem, recv_sem=recv_sem,
        device_id={"seq": peer}, device_id_type=MESH).start()


def each(count, body):
    def step(t, carry):
        body(t)
        return carry

    lax.fori_loop(0, count, step, 0)


def band(index, rows):
    return pl.ds(pl.multiple_of(index * rows, 16), rows)


ORDERS = ((2, 4), (4, 2))


def layer(
    n, tok, cot_in, taps, gw, lead, trail,
    mixed_out, g_tok_out, g_conv, g_gate, g_first, g_trail,
    cot, mixed, g_tok, halo, hbuf, w, part, r1, r2, r3, r4, conv, sa, ra, sb, rb, sc, rc, sd, rd, dcv, dg, gate,
    tok_t, lead_m, lead_t, trail_m, trail_t, cp, p1, s2, p2,
    a_s, a_r, b_s, b_r, c_s, c_r, d_s, d_r, t_s, t_r, hs, hr, p_s, p_r, z_s, z_r,
    w_s, w_r, g_s, g_r, in_s, m_s, o_s,
):
    me = lax.axis_index("seq")
    right, left = lax.rem(me + 1, n), lax.rem(me + n - 1, n)
    rows, width = tok.shape
    blocks, size = lead.shape[0], lead.shape[1]
    per = size // n
    piece = blocks * per
    cw = width // CHUNKS
    others = (n - 1) * piece
    own = width // n
    teams, group = n // 8, 8
    mine, team = lax.rem(me, group), me // group
    core = lax.rem(me, 2)

    def bit_of(bit):
        return (me // bit) % 2

    def gather_teams():
        for h in range(CHUNKS):
            at = pl.ds(h * cw, cw)
            w[h, band(me, own), :] = gw[:, at]
            for t in range(1, teams):
                hop(gw.at[:, at], w.at[h, band(me, own)], w_s.at[h, 0], w_r.at[h, 0],
                    lax.rem(me + t * group, n))

    def gather_step(h, stage):
        first, second = ORDERS[h]
        settle(w.at[h, pl.ds(0, (teams - 1) * own if stage == 1 else (teams << (stage - 2)) * own)],
               w_r.at[h, stage - 1])
        bit = (first, second, 1)[stage - 1]
        spans = 1 << (stage - 1)

        def body(t):
            z, v = t // spans, t % spans
            if stage == 1:
                inner = mine
            elif stage == 2:
                inner = mine - bit_of(first) * first + v * first
            else:
                inner = core + 2 * v
            d = z * group + inner
            hop(w.at[h, band(d, own)], w.at[h, band(d, own)], w_s.at[h, stage],
                w_r.at[h, stage], flipped(me, bit))

        each(teams * spans, body)

    def piece_of(h, stage, t, keep):
        first, second = ORDERS[h]
        if stage == 0:
            return 2 * t + (core if keep else 1 - core)
        mark = bit_of(first)
        if stage == 1:
            z, v = t // 2, t % 2
            return z * group + core + v * second + (mark if keep else 1 - mark) * first
        far = bit_of(second)
        return t * group + core + mark * first + (far if keep else 1 - far) * second

    landing = (r1, r2, r3)

    def scatter_step(h, stage):
        count = n >> (stage + 1)
        peer = flipped(me, (1, *ORDERS[h])[stage])

        def body(t):
            hop(part.at[h, band(piece_of(h, stage, t, False), own)],
                landing[stage].at[h, band(t, own)], g_s.at[h, stage], g_r.at[h, stage], peer)

        each(count, body)

    def scatter_sum(h, stage):
        count = n >> (stage + 1)
        settle(landing[stage].at[h], g_r.at[h, stage])

        def body(t):
            at = band(piece_of(h, stage, t, True), own)
            got = landing[stage][h, band(t, own), :].astype(F32)
            part[h, at, :] = (part[h, at, :].astype(F32) + got).astype(BF)

        each(count, body)

    def scatter_teams(h):
        r4[h, band(team, own), :] = part[h, band(me, own), :]
        for t in range(1, teams):
            peer = lax.rem(me + t * group, n)
            hop(part.at[h, band(peer, own)], r4.at[h, band(team, own)], g_s.at[h, 3],
                g_r.at[h, 3], peer)

    def leaving(src, dst, k, sem):
        at = pl.ds(k * cw, cw)
        return pltpu.make_async_copy(src.at[:, at], dst.at[:, at], sem.at[k])

    barrier = greet(me, n)
    fetch = pltpu.make_async_copy(cot_in, cot, in_s.at[0])
    fetch.start()
    r, c = iotas(rows, rows)
    flat = jnp.concatenate([lead[a] for a in range(blocks)], axis=0)
    turned = mm(natural_order(rows, blocks, per, True), flat).astype(BF)
    wide = jnp.concatenate([turned] * blocks, axis=1)
    lead_m[...] = jnp.where((r // per) % blocks == c // size, wide, jnp.zeros_like(wide))

    def taps_over(at, prev, x, nxt):
        return (taps[0:1, at] * prev + taps[1:2, at] * x + taps[2:3, at] * nxt).astype(BF)

    for k in range(CHUNKS):
        at = pl.ds(k * cw, cw)
        x = tok[:, at].astype(F32)
        none = jnp.zeros((1, cw), F32)
        prev, nxt = shifted(x, none, none)
        conv[k] = taps_over(at, prev, x, nxt)
    pl.semaphore_wait(barrier, n - 1)
    hop(tok.at[pl.ds(rows - 16, 16)], halo.at[0], t_s.at[0], t_r.at[0], right)
    hop(tok.at[pl.ds(0, 16)], halo.at[1], t_s.at[1], t_r.at[1], left)
    gather_teams()
    for side in range(2):
        settle(halo.at[side], t_r.at[side])

    def sides(k):
        at = pl.ds(k * cw, cw)
        before = halo[0, :, at].astype(F32)[15:16]
        after = halo[1, :, at].astype(F32)[0:1]
        before = jnp.where(me == 0, jnp.zeros_like(before), before)
        after = jnp.where(me == n - 1, jnp.zeros_like(after), after)
        return before, after

    def around(k):
        at = pl.ds(k * cw, cw)
        x = tok[:, at].astype(F32)
        prev, nxt = shifted(x, *sides(k))
        return prev, x, nxt

    for k in range(CHUNKS):
        at = pl.ds(k * cw, cw)
        edge = lax.broadcasted_iota(jnp.int32, (16, cw), 0)
        for first, row in ((0, 0), (rows - 16, 15)):
            slab = pl.ds(first, 16)
            x = tok[slab, at].astype(F32)
            prev, nxt = shifted(x, *sides(k))
            fixed = taps_over(at, prev, x, nxt).astype(F32)
            conv[k, slab, :] = jnp.where(edge == row, fixed, conv[k, slab, :].astype(F32)).astype(BF)
        sa[k] = mm(lead_m[...], conv[k]).astype(BF)
        spread(me, n, k, sa, ra, a_s, a_r, piece)
    flat = jnp.concatenate([trail[j] for j in range(per)], axis=0)
    turned = mm(inner_first(rows, per, True), flat).astype(BF)
    er, ec = iotas(size, rows)
    wide = mm(turned, one_hot(ec // per == er)).astype(BF)
    trail_m[...] = jnp.where(r % per == c % per, wide, jnp.zeros_like(wide))
    for h in range(CHUNKS):
        gather_step(h, 1)
    trail_t[...] = trail_m[...].T
    lead_t[...] = lead_m[...].T
    tok_t[...] = tok[...].T
    for h in range(CHUNKS):
        gather_step(h, 2)
    for k in range(CHUNKS):
        settle(ra.at[k, pl.ds(0, others)], a_r.at[k])
        sb[k] = mm(trail_m[...], ra[k]).astype(BF)
        spread(me, n, k, sb, rb, b_s, b_r, piece)
        gather_step(k, 3)
    order_t = natural_order(rows, blocks, per, True)
    fetch.wait()
    for k in range(CHUNKS):
        at = pl.ds(k * cw, cw)
        settle(w.at[k, pl.ds(0, n // 2 * own)], w_r.at[k, 3])
        gate[k] = mm(tok[...], w[k])
        d_mon = (cot[:, at].astype(F32) * gate[k]).astype(BF)
        sc[k] = mm(order_t, d_mon).astype(BF)
        spread(me, n, k, sc, rc, c_s, c_r, piece)
    order = natural_order(rows, blocks, per)
    strip = width // 4
    for k in range(CHUNKS):
        at = pl.ds(k * cw, cw)
        settle(rb.at[k, pl.ds(0, others)], b_r.at[k])
        m = mm(order, rb[k]).astype(BF).astype(F32)
        mixed[:, at] = (m * gate[k]).astype(BF)
        leaving(mixed, mixed_out, k, m_s).start()
        dg[k] = (cot[:, at].astype(F32) * m).astype(BF)
        for q in range(4):
            part[k, q * strip:(q + 1) * strip, :] = mm(
                tok_t[q * strip:(q + 1) * strip, :], dg[k]).astype(BF)
        scatter_step(k, 0)
    swap = inner_first(rows, per)
    for k in range(CHUNKS):
        rb[k] = mm(swap, ra[k]).astype(BF)
    for k in range(CHUNKS):
        settle(rc.at[k, pl.ds(0, others)], c_r.at[k])
        sd[k] = mm(trail_t[...], rc[k]).astype(BF)
        spread(me, n, k, sd, rd, d_s, d_r, piece)
        if k == 0:
            for h in range(CHUNKS):
                scatter_sum(h, 0)
                scatter_step(h, 1)
    for k in range(CHUNKS):
        back = mm_t(dg[0], w[0, k * cw:(k + 1) * cw, :])
        for h in range(1, CHUNKS):
            back = back + mm_t(dg[h], w[h, k * cw:(k + 1) * cw, :])
        gate[k] = back
    for k in range(CHUNKS):
        scatter_sum(k, 1)
        scatter_step(k, 2)
    for k in range(CHUNKS):
        turned = mm(swap, rc[k]).astype(BF)
        for j in range(per):
            term = mm_t(turned[j * size:(j + 1) * size], rb[k, pl.ds(j * size, size), :])
            g_trail[j] = term if k == 0 else g_trail[j] + term
    for k in range(CHUNKS):
        scatter_sum(k, 2)
        scatter_teams(k)
    for k in range(CHUNKS):
        settle(rd.at[k, pl.ds(0, others)], d_r.at[k])
        d = mm(lead_t[...], rd[k]).astype(BF)
        dcv[k] = d
        hop(dcv.at[k, pl.ds(rows - 16, 16)], hbuf.at[0, k], hs.at[0, k], hr.at[0, k], right)
        hop(dcv.at[k, pl.ds(0, 16)], hbuf.at[1, k], hs.at[1, k], hr.at[1, k], left)
        d = d.astype(F32)
        cp[k] = jnp.concatenate(
            [jnp.sum(d * v, axis=0, keepdims=True) for v in around(k)]
            + [jnp.zeros((5, cw), F32)], axis=0)
        p1[k, mine] = cp[k]
        for t in range(1, group):
            hop(cp.at[k], p1.at[k, mine], p_s.at[k], p_r.at[k],
                team * group + lax.rem(mine + t, group))
        turned = mm(order, rd[k]).astype(BF)
        for a in range(blocks):
            term = mm_t(turned[a * size:(a + 1) * size], conv[k, pl.ds(a * size, size), :])
            g_first[a] = term if k == 0 else g_first[a] + term
    for k in range(CHUNKS):
        settle(p1.at[k, pl.ds(0, group - 1)], p_r.at[k])
        total = p1[k, 0]
        for t in range(1, group):
            total = total + p1[k, t]
        s2[k] = total
        p2[k, team] = total
        for t in range(1, teams):
            hop(s2.at[k], p2.at[k, team], z_s.at[k], z_r.at[k], lax.rem(me + t * group, n))
    for k in range(CHUNKS):
        at = pl.ds(k * cw, cw)
        for side in range(2):
            settle(hbuf.at[side, k], hr.at[side, k])
        before = hbuf[0, k].astype(F32)[15:16]
        after = hbuf[1, k].astype(F32)[0:1]
        before = jnp.where(me == 0, jnp.zeros_like(before), before)
        after = jnp.where(me == n - 1, jnp.zeros_like(after), after)
        d = dcv[k].astype(F32)
        prev, nxt = shifted(d, before, after)
        back = taps[0:1, at] * nxt + taps[1:2, at] * d + taps[2:3, at] * prev
        g_tok[:, at] = (back + gate[k]).astype(BF)
        leaving(g_tok, g_tok_out, k, o_s).start()
    for k in range(CHUNKS):
        at = pl.ds(k * cw, cw)
        settle(r4.at[k, pl.ds(0, (teams - 1) * own)], g_r.at[k, 3])
        total = r4[k, pl.ds(0, own), :].astype(F32)
        for t in range(1, teams):
            total = total + r4[k, pl.ds(t * own, own), :].astype(F32)
        g_gate[:, at] = total
        settle(p2.at[k, pl.ds(0, teams - 1)], z_r.at[k])
        total = p2[k, 0]
        for t in range(1, teams):
            total = total + p2[k, t]
        g_conv[:, at] = total[0:3]
    for side in range(2):
        settle(halo.at[side], t_s.at[side])
    for k in range(CHUNKS):
        leaving(mixed, mixed_out, k, m_s).wait()
        leaving(g_tok, g_tok_out, k, o_s).wait()
        for buf, sem in ((sa, a_s), (sb, b_s), (sc, c_s), (sd, d_s)):
            settle(buf.at[k, pl.ds(0, others)], sem.at[k])
        for stage in range(4):
            count = (teams - 1) if stage == 0 else teams << (stage - 1)
            settle(w.at[k, pl.ds(0, count * own)], w_s.at[k, stage])
            count = (teams - 1) if stage == 3 else n >> (stage + 1)
            settle(part.at[k, pl.ds(0, count * own)], g_s.at[k, stage])
        settle(p1.at[k, pl.ds(0, group - 1)], p_s.at[k])
        settle(p2.at[k, pl.ds(0, teams - 1)], z_s.at[k])
        for side in range(2):
            settle(hbuf.at[side, k], hs.at[side, k])


def handed_on(*refs):
    half = len(refs) // 2
    for src, dst in zip(refs[:half], refs[half:]):
        dst[...] = src[...]


def shards(n, tokens, cotangent, taps, gate_weight, lead, trail):
    features, grad_out = tokens[0], cotangent[0]
    rows, width = features.shape
    cw = width // CHUNKS
    own = width // n
    sds = jax.ShapeDtypeStruct
    vmem = pl.BlockSpec(memory_space=pltpu.VMEM)
    dma = pltpu.SemaphoreType.DMA
    block = pltpu.VMEM((CHUNKS, rows, cw), BF)
    square = pltpu.VMEM((rows, rows), BF)
    whole = pltpu.VMEM((CHUNKS, width, cw), BF)

    def pieces(count):
        return pltpu.VMEM((CHUNKS, count * own, cw), BF)

    def tails(count):
        return pltpu.VMEM((CHUNKS, count, 8, cw), F32)

    anywhere = pl.BlockSpec(memory_space=pl.ANY)
    shapes = [sds((rows, width), BF), sds((rows, width), BF), sds((3, width), F32),
              sds((own, width), F32), sds(lead.shape, F32), sds(trail.shape, F32)]
    results = pl.pallas_call(
        functools.partial(layer, n),
        out_shape=shapes,
        in_specs=[vmem, anywhere] + [vmem] * 4,
        out_specs=[anywhere] * 2 + [vmem] * 4,
        scratch_shapes=[pltpu.VMEM((rows, width), BF)] * 3 + [pltpu.VMEM((2, 16, width), BF), pltpu.VMEM((2, CHUNKS, 16, cw), BF),
                        whole, whole, pieces(n // 2), pieces(n // 4), pieces(n // 8),
                        pieces(n // 8)]
        + [block] * 11
        + [pltpu.VMEM((CHUNKS, rows, cw), F32), pltpu.VMEM((width, rows), BF)]
        + [square] * 4
        + [pltpu.VMEM((CHUNKS, 8, cw), F32), tails(8), pltpu.VMEM((CHUNKS, 8, cw), F32),
           tails(n // 8)]
        + [dma((CHUNKS,))] * 8 + [dma((2,))] * 2 + [dma((2, CHUNKS))] * 2
        + [dma((CHUNKS,))] * 4 + [dma((CHUNKS, 4))] * 4 + [dma((1,)), dma((CHUNKS,)), dma((CHUNKS,))],
        compiler_params=pltpu.CompilerParams(
            collective_id=0, has_side_effects=True, vmem_limit_bytes=LIMIT),
        cost_estimate=pl.CostEstimate(
            flops=12 * rows * width * width, bytes_accessed=10_000_000, transcendentals=0),
        name="layer",
    )(features, grad_out, taps, gate_weight, lead, trail)

    steps = lead.shape[0]
    rows_of = pl.BlockSpec((rows // steps, width), lambda i: (i, 0))
    same = pl.BlockSpec((3, width), lambda i: (0, 0))
    all_own = pl.BlockSpec((own, width), lambda i: (0, 0))
    lead_of = pl.BlockSpec((1,) + lead.shape[1:], lambda i: (i, 0, 0))
    trail_of = pl.BlockSpec((trail.shape[0] // steps,) + trail.shape[1:], lambda i: (i, 0, 0))
    tiles = [rows_of, rows_of, same, all_own, lead_of, trail_of]
    mixed, grad_tokens, grad_conv, grad_gate, grad_first, grad_trail = pl.pallas_call(
        handed_on,
        grid=(steps,),
        out_shape=shapes,
        in_specs=tiles,
        out_specs=tiles,
        compiler_params=pltpu.CompilerParams(vmem_limit_bytes=LIMIT),
        name="handed_on",
    )(*results)

    grad_conv, grad_gate, grad_first, grad_trail = lax.psum(
        (grad_conv, grad_gate, grad_first, grad_trail), "dp")
    return mixed[None], grad_tokens[None], grad_conv, grad_gate, grad_first, grad_trail


def solution(mesh):
    seq = P("dp", "seq", None)
    specs = (seq, seq, P(), P("seq", None), P("seq", None, None), P("seq", None, None))
    return jax.shard_map(
        functools.partial(shards, mesh.shape["seq"]),
        mesh=mesh,
        in_specs=specs,
        out_specs=specs,
        check_vma=False,
    )
```
